32 devices in a mesh: sta: 8 (over y, x, core), freq: 4 (over z).
Axes of the slice: x: 2, y: 2, z: 4, core: 2. Of those that a mesh axis runs over, the one named last changes fastest.
Arguments:
- records: bfloat16 [1024, 128, 512], P('sta', 'freq'), may hold values from -6 to 6
- available: int32 [1024, 128], P('sta', 'freq'), may hold values 0 or 1
Outputs:
- cross_gram: bfloat16 [2, 128, 1024, 1024], P(None, 'freq', 'sta')
The draws below stay inside these ranges and needn't reach their ends.
All inputs are finite; a program needn't handle non-finite values. No bound on the sum of `available` on one device may be relied on, other than what follows from the above.
Results may differ from the reference program's by a relative error of at most 0.0056.
Values may be sent and summed in bfloat16 or wider, within the bound.
A program may use at most 192 MiB of HBM per device.

```python
import jax
import jax.numpy as jnp
from jax import lax

FFT_LEN = 512
BINS = 128
BAND_LO = 16
STATIONS = 1024
SEGS = 128


def plant(array, stream_key, smallest, high):
    longest = array.shape.index(max(array.shape))
    spots = []
    for shift in (0, 1):
        where = [jax.random.randint(jax.random.fold_in(stream_key, axis), (), 0, length) for axis, length in enumerate(array.shape)]
        where[longest] = (where[longest] + shift) % array.shape[longest]
        spots.append(tuple(where))
    return array.at[spots[0]].set(smallest).at[spots[1]].set(high)


def shard_levels(key, dims, cuts, smallest, largest):
    factor_of, own = 1.0, jax.random.fold_in(key, 6)
    for axis_at, blocks in cuts:
        steps = jnp.exp(jax.random.uniform(jax.random.fold_in(own, axis_at), (blocks,), jnp.float32, smallest / len(cuts), largest / len(cuts)))
        factor_of = factor_of * jnp.repeat(steps, dims[axis_at] // blocks).reshape([-1 if axis == axis_at else 1 for axis in range(len(dims))])
    return factor_of


def centred(key, extent, spread, bound, split=(), held_as=jnp.bfloat16):
    entries = jax.random.normal(key, extent, jnp.float32) * spread
    if len(split) > 0:
        entries = shard_levels(key, extent, split, -0.22, 0.18) * entries
    return jnp.clip(entries, min=-bound, max=bound).astype(held_as)


def setup_inputs(seed: int = 0) -> dict:
    streams_of = jax.random.split(jax.random.key(seed), 3)
    return {
        "records": centred(streams_of[0], (STATIONS, SEGS, FFT_LEN), 1.0, 6.0, ((0, 8), (1, 4))),
        "available": plant((jax.random.randint(streams_of[1], (STATIONS, SEGS), 0, 4) < 3).astype(jnp.int32), jax.random.fold_in(streams_of[1], 1), 0, 1),
    }


def whiten(records, available):
    sample_pos = jnp.arange(FFT_LEN, dtype=jnp.float32)
    window_taper = 0.5 - 0.5 * jnp.cos(2.0 * jnp.pi * sample_pos / FFT_LEN)
    tapered = records.astype(jnp.float32) * window_taper
    spectrum = jnp.fft.rfft(tapered, axis=-1)[..., BAND_LO:BAND_LO + BINS]
    real_part = jnp.real(spectrum)
    imag_part = jnp.imag(spectrum)
    power = lax.optimization_barrier(jnp.mean(real_part * real_part + imag_part * imag_part, axis=-1, keepdims=True))
    weight = available.astype(jnp.float32)[..., None] / jnp.sqrt(power + 1e-05)
    return ((real_part * weight).astype(jnp.bfloat16), (imag_part * weight).astype(jnp.bfloat16))

def reference(records, available):
    real_white, imag_white = whiten(records, available)
    real_bins = jnp.transpose(real_white, (2, 0, 1))
    imag_bins = jnp.transpose(imag_white, (2, 0, 1))
    highest = lax.Precision.HIGHEST

    def one_bin(pair):
        real_rows = pair[0].astype(jnp.float32)
        imag_rows = pair[1].astype(jnp.float32)
        both_real = jnp.dot(real_rows, real_rows.T, precision=highest, preferred_element_type=jnp.float32)
        both_imag = jnp.dot(imag_rows, imag_rows.T, precision=highest, preferred_element_type=jnp.float32)
        imag_real = jnp.dot(imag_rows, real_rows.T, precision=highest, preferred_element_type=jnp.float32)
        real_imag = jnp.dot(real_rows, imag_rows.T, precision=highest, preferred_element_type=jnp.float32)
        gram_real = ((both_real + both_imag) / SEGS).astype(jnp.bfloat16)
        gram_imag = ((imag_real - real_imag) / SEGS).astype(jnp.bfloat16)
        return (gram_real, gram_imag)
    gram_real, gram_imag = lax.map(one_bin, (real_bins, imag_bins))
    return jnp.stack([gram_real, gram_imag])
```

```python
import functools

import jax
import jax.numpy as jnp
import ml_dtypes
import numpy as np
from jax import lax
from jax.experimental import pallas as pl
from jax.experimental.pallas import tpu as pltpu
from jax.sharding import PartitionSpec as P

FFT_LEN = 512
BINS = 128
BAND_LO = 16
PARTS = 2
MESH = pl.DeviceIdType.MESH
MIB = 1 << 20


def spectra_tables():
    t = np.arange(FFT_LEN)
    window = 0.5 - 0.5 * np.cos(2.0 * np.pi * t / FFT_LEN)
    phase = (np.arange(BAND_LO, BAND_LO + BINS)[:, None] * t[None, :] % FFT_LEN) * (2.0 * np.pi / FFT_LEN)
    table = np.concatenate([np.cos(phase), -np.sin(phase)], axis=0) * window
    high = table.astype(ml_dtypes.bfloat16)
    low = (table - high.astype(np.float64)).astype(ml_dtypes.bfloat16)
    return high, low


def exchange_kernel(
    n_sta, n_freq,
    records, avail, high, low, gathered,
    rec, wide, spread, own, rec_sem, keep_sem, zsend, zrecv, send, recv,
):
    me = lax.axis_index("sta")
    z = lax.axis_index("freq")
    stations, part_segs = rec.shape[1], rec.shape[2]
    rows = 2 * part_segs
    bins = BINS // n_freq
    mask_bits = [1 << k for k in range(n_sta.bit_length() - 1)]
    far_bits = mask_bits[1:]

    loads = []
    for part in range(PARTS):
        load = pltpu.make_async_copy(
            records.at[:, pl.ds(part * part_segs, part_segs), :], rec.at[part], rec_sem.at[part]
        )
        load.start()
        loads.append(load)

    barrier = pltpu.get_barrier_semaphore()
    for bit in mask_bits:
        pl.semaphore_signal(barrier, inc=1, device_id=(me ^ bit, z), device_id_type=MESH)
    for step in range(1, n_freq):
        pl.semaphore_signal(barrier, inc=1, device_id=(me, z ^ step), device_id_type=MESH)

    def transform(part):
        loads[part].wait()

        def widen(block, carry):
            first = pl.multiple_of(block * 16, 16)
            for col in range(FFT_LEN // 128):
                values = rec[part, pl.ds(first, 16), :, pl.ds(col * 128, 128)]
                wide[col, pl.ds(pl.multiple_of(first * part_segs, 256), 16 * part_segs), :] = (
                    values.astype(jnp.float32).reshape(16 * part_segs, 128)
                )
            return carry

        lax.fori_loop(0, stations // 16, widen, 0)

        for pair in range(part_segs // 2):
            pieces = []
            for seg in (2 * pair, 2 * pair + 1):
                pieces.append(jnp.concatenate(
                    [wide[col, pl.ds(seg, stations, stride=part_segs), :] for col in range(FFT_LEN // 128)], axis=1
                ))
            x = jnp.concatenate(pieces, axis=0).astype(jnp.bfloat16)
            contract = (((1,), (1,)), ((), ()))
            spectra = lax.dot_general(high[...], x, contract, preferred_element_type=jnp.float32)
            spectra += lax.dot_general(low[...], x, contract, preferred_element_type=jnp.float32)
            power = jnp.sum(spectra * spectra, axis=0, keepdims=True) * (1.0 / BINS)
            for k, seg in enumerate((2 * pair, 2 * pair + 1)):
                lanes = slice(k * stations, (k + 1) * stations)
                usable = avail[pl.ds(part * part_segs + seg, 1), :]
                weight = usable / jnp.sqrt(power[:, lanes] + 1e-05)
                white = spectra[:, lanes] * weight
                spread[pl.ds(seg, BINS, stride=rows), :] = white[:BINS]
                spread[pl.ds(part_segs + seg, BINS, stride=rows), :] = white[BINS:]

        for dest in range(n_freq):
            block = spread[dest * bins * rows:(dest + 1) * bins * rows, :]
            own[dest, part] = block.astype(jnp.bfloat16).reshape(bins, rows, 128)

    def orders(part):
        return far_bits if part % 2 == 0 else far_bits[::-1]

    def piece(step, part, mask):
        return gathered.at[me ^ mask, z ^ step, part]

    def forward(step, part, mask, bit):
        src = own.at[z, part] if mask == 0 and step == 0 else piece(step, part, mask)
        return pltpu.make_async_remote_copy(
            src_ref=src, dst_ref=piece(step, part, mask),
            send_sem=send.at[step * PARTS + part, mask ^ bit], recv_sem=recv.at[step * PARTS + part, mask ^ bit],
            device_id=(me ^ bit, z), device_id_type=MESH,
        )

    def arrival(step, part, mask):
        here = piece(step, part, mask)
        return pltpu.make_async_remote_copy(
            src_ref=here, dst_ref=here,
            send_sem=send.at[step * PARTS + part, mask], recv_sem=recv.at[step * PARTS + part, mask],
            device_id=(me ^ (mask & -mask), z), device_id_type=MESH,
        )

    def cross(step, part):
        return pltpu.make_async_remote_copy(
            src_ref=own.at[z ^ step, part], dst_ref=gathered.at[me, z, part],
            send_sem=zsend.at[step * PARTS + part], recv_sem=zrecv.at[step * PARTS + part],
            device_id=(me, z ^ step), device_id_type=MESH,
        )

    def crossed(step, part):
        here = piece(step, part, 0)
        return pltpu.make_async_remote_copy(
            src_ref=here, dst_ref=here,
            send_sem=zsend.at[step * PARTS + part], recv_sem=zrecv.at[step * PARTS + part],
            device_id=(me, z ^ step), device_id_type=MESH,
        )

    started = []

    def push(step, part, mask):
        order = orders(part)
        last = max([order.index(bit) for bit in order if mask & bit], default=-1)
        for bit in order[last + 1:] + [1]:
            copy = forward(step, part, mask, bit)
            copy.start()
            started.append(copy)

    keeps = []
    for part in range(PARTS):
        transform(part)
        if part == 0:
            pl.semaphore_wait(barrier, len(mask_bits) + n_freq - 1)
        push(0, part, 0)
        for step in range(1, n_freq):
            copy = cross(step, part)
            copy.start()
            started.append(copy)
        keep = pltpu.make_async_copy(own.at[z, part], gathered.at[me, z, part], keep_sem.at[part])
        keep.start()
        keeps.append(keep)

    far_masks = [mask for mask in range(2, n_sta, 2)]
    count = n_freq * PARTS
    depth = len(far_bits)
    for turn in range(PARTS, count + depth + 1):
        for lag in range(depth + 1):
            index = turn - lag
            if lag == 0 and index < count:
                step, part = divmod(index, PARTS)
                crossed(step, part).wait_recv()
                push(step, part, 0)
            lower = 0 if turn == PARTS else index
            for slot in range(lower, index + 1):
                if lag > 0 and 0 <= slot < count:
                    step, part = divmod(slot, PARTS)
                    for mask in far_masks:
                        if bin(mask).count("1") == lag:
                            arrival(step, part, mask).wait_recv()
                            push(step, part, mask)

    for slot in range(count):
        step, part = divmod(slot, PARTS)
        for mask in range(1, n_sta, 2):
            arrival(step, part, mask).wait_recv()
    for keep in keeps:
        keep.wait()
    for copy in started:
        copy.wait_send()


def gram_kernel(per_step, scale, panel, out):
    me = lax.axis_index("sta")
    n_sta, n_freq, parts, _, rows, _ = panel.shape
    half = rows // 2
    places = [(z, part) for z in range(n_freq) for part in range(parts)]
    for b in range(per_step):
        plain, turned = [], []
        for z, part in places:
            block = panel[me, z, part, b] * scale
            plain.append(block)
            turned += [block[half:], -block[:half]]
        mine = jnp.concatenate([jnp.concatenate(plain, axis=0), jnp.concatenate(turned, axis=0)], axis=1)
        every = jnp.concatenate(
            [jnp.concatenate([panel[j, z, part, b] for z, part in places], axis=0) for j in range(n_sta)], axis=1
        )
        gram = lax.dot_general(mine, every, (((0,), (0,)), ((), ())), preferred_element_type=jnp.float32)
        gram = gram.astype(jnp.bfloat16)
        stations = out.shape[2]
        out[0, b] = gram[:stations]
        out[1, b] = gram[stations:]


def shards(n_sta, n_freq, records, available):
    stations, segments, samples = records.shape
    part_segs = segments // PARTS
    rows = 2 * part_segs
    bins = BINS // n_freq
    avail = available.astype(jnp.float32).T
    high, low = spectra_tables()
    vmem = pl.BlockSpec(memory_space=pltpu.VMEM)
    count = n_freq * PARTS
    gathered = pl.pallas_call(
        functools.partial(exchange_kernel, n_sta, n_freq),
        out_shape=jax.ShapeDtypeStruct((n_sta, n_freq, PARTS, bins, rows, stations), jnp.bfloat16),
        in_specs=[pl.BlockSpec(memory_space=pl.ANY), vmem, vmem, vmem],
        out_specs=pl.BlockSpec(memory_space=pl.ANY),
        scratch_shapes=[
            pltpu.VMEM((PARTS, stations, part_segs, samples), jnp.bfloat16),
            pltpu.VMEM((samples // 128, stations * part_segs, 128), jnp.float32),
            pltpu.VMEM((BINS * rows, stations), jnp.float32),
            pltpu.VMEM((n_freq, PARTS, bins, rows, stations), jnp.bfloat16),
            pltpu.SemaphoreType.DMA((PARTS,)),
            pltpu.SemaphoreType.DMA((PARTS,)),
            pltpu.SemaphoreType.DMA((count,)),
            pltpu.SemaphoreType.DMA((count,)),
            pltpu.SemaphoreType.DMA((count, n_sta)),
            pltpu.SemaphoreType.DMA((count, n_sta)),
        ],
        compiler_params=pltpu.CompilerParams(
            collective_id=0, has_side_effects=True, vmem_limit_bytes=20 * MIB
        ),
        name="spectra_exchange",
    )(records, avail, jnp.asarray(high), jnp.asarray(low))

    per_step = 4
    scale = 1.0 / (segments * n_freq)
    return pl.pallas_call(
        functools.partial(gram_kernel, per_step, scale),
        out_shape=jax.ShapeDtypeStruct((2, bins, stations, stations * n_sta), jnp.bfloat16),
        grid=(bins // per_step,),
        in_specs=[pl.BlockSpec((n_sta, n_freq, PARTS, per_step, rows, stations), lambda i: (0, 0, 0, i, 0, 0))],
        out_specs=pl.BlockSpec((2, per_step, stations, stations * n_sta), lambda i: (0, i, 0, 0)),
        compiler_params=pltpu.CompilerParams(vmem_limit_bytes=40 * MIB),
        name="gram",
    )(gathered)


def solution(mesh):
    in_specs = (P("sta", "freq", None), P("sta", "freq"))
    out_specs = P(None, "freq", "sta", None)
    body = functools.partial(shards, mesh.shape["sta"], mesh.shape["freq"])
    return jax.shard_map(body, mesh=mesh, in_specs=in_specs, out_specs=out_specs, check_vma=False)
```

```python
import functools

import jax
import jax.numpy as jnp
import ml_dtypes
import numpy as np
from jax import lax
from jax.experimental import pallas as pl
from jax.experimental.pallas import tpu as pltpu
from jax.sharding import PartitionSpec as P

FFT_LEN = 512
BINS = 128
BAND_LO = 16
PARTS = 4
TERMS = 3
LOADS = 2
MESH = pl.DeviceIdType.MESH
MIB = 1 << 20


def spectra_tables():
    t = np.arange(FFT_LEN)
    window = 0.5 - 0.5 * np.cos(2.0 * np.pi * t / FFT_LEN)
    phase = (np.arange(BAND_LO, BAND_LO + BINS)[:, None] * t[None, :] % FFT_LEN) * (2.0 * np.pi / FFT_LEN)
    table = np.concatenate([np.cos(phase), -np.sin(phase)], axis=0) * window
    terms = []
    for _ in range(TERMS):
        terms.append(table.astype(ml_dtypes.bfloat16))
        table = table - terms[-1].astype(np.float64)
    return np.concatenate(terms, axis=0)


def exchange_kernel(
    n_sta, n_freq,
    records, available, table, gathered,
    rec, avail, terms, wide, spread, own, rec_sem, keep_sem, zsend, zrecv, send, recv,
):
    me = lax.axis_index("sta")
    z = lax.axis_index("freq")
    stations, load_segs = rec.shape[1], rec.shape[2]
    part_segs = load_segs * LOADS // PARTS
    rows = 2 * part_segs
    bins = BINS // n_freq
    mask_bits = [1 << k for k in range(n_sta.bit_length() - 1)]
    far_bits = mask_bits[1:]

    loads = [pltpu.make_async_copy(table, terms, rec_sem.at[LOADS])]
    loads.append(pltpu.make_async_copy(available, avail, rec_sem.at[LOADS + 1]))
    for k in range(LOADS):
        source = records.at[:, pl.ds(k * load_segs, load_segs), :]
        loads.append(pltpu.make_async_copy(source, rec.at[k], rec_sem.at[k]))
    for load in loads:
        load.start()

    barrier = pltpu.get_barrier_semaphore()
    for bit in mask_bits:
        pl.semaphore_signal(barrier, inc=1, device_id=(me ^ bit, z), device_id_type=MESH)
    for step in range(1, n_freq):
        pl.semaphore_signal(barrier, inc=1, device_id=(me, z ^ step), device_id_type=MESH)

    def widen(k):
        def some(block, carry):
            first = pl.multiple_of(block * 16, 16)
            for col in range(FFT_LEN // 128):
                values = rec[k, pl.ds(first, 16), :, pl.ds(col * 128, 128)]
                wide[col, pl.ds(pl.multiple_of(first * load_segs, 256), 16 * load_segs), :] = (
                    values.astype(jnp.float32).reshape(16 * load_segs, 128)
                )
            return carry

        lax.fori_loop(0, stations // 16, some, 0)

    def transform(part):
        offset = part * part_segs % load_segs
        for pair in range(part_segs // 2):
            pieces = []
            for seg in (2 * pair, 2 * pair + 1):
                pieces.append(jnp.concatenate(
                    [wide[col, pl.ds(offset + seg, stations, stride=load_segs), :] for col in range(FFT_LEN // 128)],
                    axis=1,
                ))
            x = jnp.concatenate(pieces, axis=0).astype(jnp.bfloat16)
            contract = (((1,), (1,)), ((), ()))
            sums = lax.dot_general(terms[...], x, contract, preferred_element_type=jnp.float32)
            spectra = sums[(TERMS - 1) * 2 * BINS:]
            for term in range(TERMS - 2, -1, -1):
                spectra = spectra + sums[term * 2 * BINS:(term + 1) * 2 * BINS]
            power = jnp.sum(spectra * spectra, axis=0, keepdims=True) * (1.0 / BINS)
            for k, seg in enumerate((2 * pair, 2 * pair + 1)):
                lanes = slice(k * stations, (k + 1) * stations)
                usable = avail[pl.ds(part * part_segs + seg, 1), :].astype(jnp.float32)
                weight = usable / jnp.sqrt(power[:, lanes] + 1e-05)
                white = spectra[:, lanes] * weight
                spread[pl.ds(seg, BINS, stride=rows), :] = white[:BINS]
                spread[pl.ds(part_segs + seg, BINS, stride=rows), :] = white[BINS:]

        for dest in range(n_freq):
            block = spread[dest * bins * rows:(dest + 1) * bins * rows, :]
            own[dest, part] = block.astype(jnp.bfloat16).reshape(bins, rows, 128)

    def orders(part):
        return far_bits if part % 2 == 0 else far_bits[::-1]

    def piece(step, part, mask):
        return gathered.at[me ^ mask, z ^ step, part]

    def forward(step, part, mask, bit):
        src = own.at[z, part] if mask == 0 and step == 0 else piece(step, part, mask)
        return pltpu.make_async_remote_copy(
            src_ref=src, dst_ref=piece(step, part, mask),
            send_sem=send.at[step * PARTS + part, mask ^ bit], recv_sem=recv.at[step * PARTS + part, mask ^ bit],
            device_id=(me ^ bit, z), device_id_type=MESH,
        )

    def arrival(step, part, mask):
        here = piece(step, part, mask)
        return pltpu.make_async_remote_copy(
            src_ref=here, dst_ref=here,
            send_sem=send.at[step * PARTS + part, mask], recv_sem=recv.at[step * PARTS + part, mask],
            device_id=(me ^ (mask & -mask), z), device_id_type=MESH,
        )

    def cross(step, part):
        return pltpu.make_async_remote_copy(
            src_ref=own.at[z ^ step, part], dst_ref=gathered.at[me, z, part],
            send_sem=zsend.at[step * PARTS + part], recv_sem=zrecv.at[step * PARTS + part],
            device_id=(me, z ^ step), device_id_type=MESH,
        )

    def crossed(step, part):
        here = piece(step, part, 0)
        return pltpu.make_async_remote_copy(
            src_ref=here, dst_ref=here,
            send_sem=zsend.at[step * PARTS + part], recv_sem=zrecv.at[step * PARTS + part],
            device_id=(me, z ^ step), device_id_type=MESH,
        )

    started = []

    def push(step, part, mask):
        order = orders(part)
        last = max([order.index(bit) for bit in order if mask & bit], default=-1)
        for bit in order[last + 1:] + [1]:
            copy = forward(step, part, mask, bit)
            copy.start()
            started.append(copy)

    keeps = []
    for part in range(PARTS):
        if part == 0:
            loads[0].wait()
            loads[1].wait()
        if part % (PARTS // LOADS) == 0:
            loads[2 + part * LOADS // PARTS].wait()
            widen(part * LOADS // PARTS)
        transform(part)
        if part == 0:
            pl.semaphore_wait(barrier, len(mask_bits) + n_freq - 1)
        push(0, part, 0)
        for step in range(1, n_freq):
            copy = cross(step, part)
            copy.start()
            started.append(copy)
        keep = pltpu.make_async_copy(own.at[z, part], gathered.at[me, z, part], keep_sem.at[part])
        keep.start()
        keeps.append(keep)

    far_masks = [mask for mask in range(2, n_sta, 2)]
    count = n_freq * PARTS
    depth = len(far_bits)
    for turn in range(PARTS, count + depth + 1):
        for lag in range(depth + 1):
            index = turn - lag
            if lag == 0 and index < count:
                step, part = divmod(index, PARTS)
                crossed(step, part).wait_recv()
                push(step, part, 0)
            lower = 0 if turn == PARTS else index
            for slot in range(lower, index + 1):
                if lag > 0 and 0 <= slot < count:
                    step, part = divmod(slot, PARTS)
                    for mask in far_masks:
                        if bin(mask).count("1") == lag:
                            arrival(step, part, mask).wait_recv()
                            push(step, part, mask)

    for slot in range(count):
        step, part = divmod(slot, PARTS)
        for mask in range(1, n_sta, 2):
            arrival(step, part, mask).wait_recv()
    for keep in keeps:
        keep.wait()
    for copy in started:
        copy.wait_send()


def gram_kernel(per_step, scale, panel, out):
    me = lax.axis_index("sta")
    n_sta, n_freq, parts, _, rows, _ = panel.shape
    half = rows // 2
    first = pl.program_id(0) * per_step
    places = [(z, part) for z in range(n_freq) for part in range(parts)]
    stations = out.shape[2]
    wide = 2 * stations
    for b in range(per_step):
        plain, turned = [], []
        for z, part in places:
            block = panel[me, z, part, first + b].astype(jnp.float32) * scale
            plain.append(block)
            turned += [block[half:], -block[:half]]
        mine = jnp.concatenate([jnp.concatenate(plain, axis=0), jnp.concatenate(turned, axis=0)], axis=1)
        mine = mine.T.astype(jnp.bfloat16)
        for j in range(0, n_sta, 2):
            other = jnp.concatenate(
                [jnp.concatenate([panel[j + k, z, part, first + b] for z, part in places], axis=0) for k in (0, 1)],
                axis=1,
            )
            gram = jnp.dot(mine, other, preferred_element_type=jnp.float32).astype(jnp.bfloat16)
            columns = slice(j * stations, j * stations + wide)
            out[0, b, :, columns] = gram[:stations]
            out[1, b, :, columns] = gram[stations:]


def shards(n_sta, n_freq, records, available):
    stations, segments, samples = records.shape
    part_segs = segments // PARTS
    rows = 2 * part_segs
    bins = BINS // n_freq
    operands = [records, available.T, jnp.asarray(spectra_tables())]
    operands = [pltpu.with_memory_space_constraint(operand, pltpu.HBM) for operand in operands]
    count = n_freq * PARTS
    gathered = pl.pallas_call(
        functools.partial(exchange_kernel, n_sta, n_freq),
        out_shape=jax.ShapeDtypeStruct((n_sta, n_freq, PARTS, bins, rows, stations), jnp.bfloat16),
        in_specs=[pl.BlockSpec(memory_space=pltpu.HBM)] * len(operands),
        out_specs=pl.BlockSpec(memory_space=pl.ANY),
        scratch_shapes=[
            pltpu.VMEM((LOADS, stations, segments // LOADS, samples), jnp.bfloat16),
            pltpu.VMEM((segments, stations), jnp.int32),
            pltpu.VMEM((TERMS * 2 * BINS, samples), jnp.bfloat16),
            pltpu.VMEM((samples // 128, stations * segments // LOADS, 128), jnp.float32),
            pltpu.VMEM((BINS * rows, stations), jnp.float32),
            pltpu.VMEM((n_freq, PARTS, bins, rows, stations), jnp.bfloat16),
            pltpu.SemaphoreType.DMA((LOADS + 2,)),
            pltpu.SemaphoreType.DMA((PARTS,)),
            pltpu.SemaphoreType.DMA((count,)),
            pltpu.SemaphoreType.DMA((count,)),
            pltpu.SemaphoreType.DMA((count, n_sta)),
            pltpu.SemaphoreType.DMA((count, n_sta)),
        ],
        compiler_params=pltpu.CompilerParams(
            collective_id=0, has_side_effects=True, vmem_limit_bytes=18 * MIB
        ),
        name="spectra_exchange",
    )(*operands)

    per_step = 4
    scale = 1.0 / (segments * n_freq)
    return pl.pallas_call(
        functools.partial(gram_kernel, per_step, scale),
        out_shape=jax.ShapeDtypeStruct((2, bins, stations, stations * n_sta), jnp.bfloat16),
        grid=(bins // per_step,),
        in_specs=[pl.BlockSpec(memory_space=pltpu.VMEM)],
        out_specs=pl.BlockSpec((2, per_step, stations, stations * n_sta), lambda i: (0, i, 0, 0)),
        compiler_params=pltpu.CompilerParams(vmem_limit_bytes=12 * MIB),
        name="gram",
    )(gathered)


def solution(mesh):
    in_specs = (P("sta", "freq", None), P("sta", "freq"))
    out_specs = P(None, "freq", "sta", None)
    body = functools.partial(shards, mesh.shape["sta"], mesh.shape["freq"])
    return jax.shard_map(body, mesh=mesh, in_specs=in_specs, out_specs=out_specs, check_vma=False)
```

```python
import functools

import jax
import jax.numpy as jnp
import ml_dtypes
import numpy as np
from jax import lax
from jax.experimental import pallas as pl
from jax.experimental.pallas import tpu as pltpu
from jax.sharding import PartitionSpec as P

FFT_LEN = 512
BINS = 128
BAND_LO = 16
PARTS = 4
TERMS = 3
LOADS = 2
AHEAD = 2
Z_AHEAD = 6
MESH = pl.DeviceIdType.MESH
MIB = 1 << 20


def spectra_tables():
    t = np.arange(FFT_LEN)
    window = 0.5 - 0.5 * np.cos(2.0 * np.pi * t / FFT_LEN)
    phase = (np.arange(BAND_LO, BAND_LO + BINS)[:, None] * t[None, :] % FFT_LEN) * (2.0 * np.pi / FFT_LEN)
    table = np.concatenate([np.cos(phase), -np.sin(phase)], axis=0) * window
    terms = []
    for _ in range(TERMS):
        terms.append(table.astype(ml_dtypes.bfloat16))
        table = table - terms[-1].astype(np.float64)
    return np.concatenate(terms, axis=0)


def exchange_kernel(
    n_sta, n_freq,
    records, available, table, gathered,
    rec, avail, terms, wide, spread, own, rec_sem, keep_sem, zsend, zrecv, send, recv,
):
    me = lax.axis_index("sta")
    z = lax.axis_index("freq")
    stations, load_segs = rec.shape[1], rec.shape[2]
    part_segs = load_segs * LOADS // PARTS
    rows = 2 * part_segs
    bins = BINS // n_freq
    mask_bits = [1 << k for k in range(n_sta.bit_length() - 1)]
    far_bits = mask_bits[1:]

    loads = [pltpu.make_async_copy(table, terms, rec_sem.at[LOADS])]
    loads.append(pltpu.make_async_copy(available, avail, rec_sem.at[LOADS + 1]))
    for k in range(LOADS):
        source = records.at[:, pl.ds(k * load_segs, load_segs), :]
        loads.append(pltpu.make_async_copy(source, rec.at[k], rec_sem.at[k]))
    for load in loads:
        load.start()

    barrier = pltpu.get_barrier_semaphore()
    for bit in mask_bits:
        pl.semaphore_signal(barrier, inc=1, device_id=(me ^ bit, z), device_id_type=MESH)
    for step in range(1, n_freq):
        pl.semaphore_signal(barrier, inc=1, device_id=(me, z ^ step), device_id_type=MESH)

    def widen(k):
        def some(block, carry):
            first = pl.multiple_of(block * 16, 16)
            for col in range(FFT_LEN // 128):
                values = rec[k, pl.ds(first, 16), :, pl.ds(col * 128, 128)]
                wide[col, pl.ds(pl.multiple_of(first * load_segs, 256), 16 * load_segs), :] = (
                    values.astype(jnp.float32).reshape(16 * load_segs, 128)
                )
            return carry

        lax.fori_loop(0, stations // 16, some, 0)

    def transform(part):
        offset = part * part_segs % load_segs
        for pair in range(part_segs // 2):
            pieces = []
            for seg in (2 * pair, 2 * pair + 1):
                pieces.append(jnp.concatenate(
                    [wide[col, pl.ds(offset + seg, stations, stride=load_segs), :] for col in range(FFT_LEN // 128)],
                    axis=1,
                ))
            x = jnp.concatenate(pieces, axis=0).astype(jnp.bfloat16)
            contract = (((1,), (1,)), ((), ()))
            sums = lax.dot_general(terms[...], x, contract, preferred_element_type=jnp.float32)
            spectra = sums[(TERMS - 1) * 2 * BINS:]
            for term in range(TERMS - 2, -1, -1):
                spectra = spectra + sums[term * 2 * BINS:(term + 1) * 2 * BINS]
            power = jnp.sum(spectra * spectra, axis=0, keepdims=True) * (1.0 / BINS)
            for k, seg in enumerate((2 * pair, 2 * pair + 1)):
                lanes = slice(k * stations, (k + 1) * stations)
                usable = avail[pl.ds(part * part_segs + seg, 1), :].astype(jnp.float32)
                weight = usable / jnp.sqrt(power[:, lanes] + 1e-05)
                white = spectra[:, lanes] * weight
                spread[pl.ds(seg, BINS, stride=rows), :] = white[:BINS]
                spread[pl.ds(part_segs + seg, BINS, stride=rows), :] = white[BINS:]

        for dest in range(n_freq):
            block = spread[dest * bins * rows:(dest + 1) * bins * rows, :]
            own[dest, part] = block.astype(jnp.bfloat16).reshape(bins, rows, 128)

    def orders(part):
        return far_bits if part % 2 == 0 else far_bits[::-1]

    def piece(step, part, mask):
        return gathered.at[me ^ mask, z ^ step, part]

    def forward(step, part, mask, bit):
        src = own.at[z, part] if mask == 0 and step == 0 else piece(step, part, mask)
        return pltpu.make_async_remote_copy(
            src_ref=src, dst_ref=piece(step, part, mask),
            send_sem=send.at[step * PARTS + part, mask ^ bit], recv_sem=recv.at[step * PARTS + part, mask ^ bit],
            device_id=(me ^ bit, z), device_id_type=MESH,
        )

    def arrival(step, part, mask):
        here = piece(step, part, mask)
        return pltpu.make_async_remote_copy(
            src_ref=here, dst_ref=here,
            send_sem=send.at[step * PARTS + part, mask], recv_sem=recv.at[step * PARTS + part, mask],
            device_id=(me ^ (mask & -mask), z), device_id_type=MESH,
        )

    def cross(step, part):
        return pltpu.make_async_remote_copy(
            src_ref=own.at[z ^ step, part], dst_ref=gathered.at[me, z, part],
            send_sem=zsend.at[step * PARTS + part], recv_sem=zrecv.at[step * PARTS + part],
            device_id=(me, z ^ step), device_id_type=MESH,
        )

    def crossed(step, part):
        here = piece(step, part, 0)
        return pltpu.make_async_remote_copy(
            src_ref=here, dst_ref=here,
            send_sem=zsend.at[step * PARTS + part], recv_sem=zrecv.at[step * PARTS + part],
            device_id=(me, z ^ step), device_id_type=MESH,
        )

    started = []

    def push(step, part, mask):
        order = orders(part)
        last = max([order.index(bit) for bit in order if mask & bit], default=-1)
        for bit in order[last + 1:] + [1]:
            copy = forward(step, part, mask, bit)
            copy.start()
            started.append(copy)

    def launch(step, part):
        copy = cross(step, part)
        copy.start()
        started.append(copy)

    keeps = []
    for part in range(PARTS):
        if part == 0:
            loads[0].wait()
            loads[1].wait()
        if part % (PARTS // LOADS) == 0:
            loads[2 + part * LOADS // PARTS].wait()
            widen(part * LOADS // PARTS)
        transform(part)
        if part == 0:
            pl.semaphore_wait(barrier, len(mask_bits) + n_freq - 1)
        push(0, part, 0)
        launch(1, part)
        keep = pltpu.make_async_copy(own.at[z, part], gathered.at[me, z, part], keep_sem.at[part])
        keep.start()
        keeps.append(keep)

    far_masks = [mask for mask in range(2, n_sta, 2)]
    count = n_freq * PARTS
    depth = len(far_bits)
    launched = 2 * PARTS
    reached = [PARTS] + [0] * depth
    for turn in range(PARTS, count + AHEAD + depth + 1):
        while launched < min(count, turn + Z_AHEAD + 1):
            launch(*divmod(launched, PARTS))
            launched += 1
        for lag in range(depth + 1):
            limit = min(count, turn + 1 - (lag + AHEAD if lag else 0))
            for slot in range(reached[lag], limit):
                step, part = divmod(slot, PARTS)
                if lag == 0:
                    crossed(step, part).wait_recv()
                    push(step, part, 0)
                else:
                    for mask in far_masks:
                        if bin(mask).count("1") == lag:
                            arrival(step, part, mask).wait_recv()
                            push(step, part, mask)
            reached[lag] = max(reached[lag], limit)
    assert min(reached) == count and launched == count

    for slot in range(count):
        step, part = divmod(slot, PARTS)
        for mask in range(1, n_sta, 2):
            arrival(step, part, mask).wait_recv()
    for keep in keeps:
        keep.wait()
    for copy in started:
        copy.wait_send()


def gram_kernel(per_step, scale, panel, out):
    me = lax.axis_index("sta")
    n_sta, n_freq, parts, _, rows, _ = panel.shape
    half = rows // 2
    first = pl.program_id(0) * per_step
    places = [(z, part) for z in range(n_freq) for part in range(parts)]
    stations = out.shape[2]
    wide = 2 * stations
    for b in range(per_step):
        plain, turned = [], []
        for z, part in places:
            block = panel[me, z, part, first + b].astype(jnp.float32) * scale
            plain.append(block)
            turned += [block[half:], -block[:half]]
        mine = jnp.concatenate([jnp.concatenate(plain, axis=0), jnp.concatenate(turned, axis=0)], axis=1)
        mine = mine.T.astype(jnp.bfloat16)
        for j in range(0, n_sta, 2):
            other = jnp.concatenate(
                [jnp.concatenate([panel[j + k, z, part, first + b] for z, part in places], axis=0) for k in (0, 1)],
                axis=1,
            )
            gram = jnp.dot(mine, other, preferred_element_type=jnp.float32).astype(jnp.bfloat16)
            columns = slice(j * stations, j * stations + wide)
            out[0, b, :, columns] = gram[:stations]
            out[1, b, :, columns] = gram[stations:]


def shards(n_sta, n_freq, records, available):
    stations, segments, samples = records.shape
    part_segs = segments // PARTS
    rows = 2 * part_segs
    bins = BINS // n_freq
    operands = [records, available.T, jnp.asarray(spectra_tables())]
    operands = [pltpu.with_memory_space_constraint(operand, pltpu.HBM) for operand in operands]
    count = n_freq * PARTS
    gathered = pl.pallas_call(
        functools.partial(exchange_kernel, n_sta, n_freq),
        out_shape=jax.ShapeDtypeStruct((n_sta, n_freq, PARTS, bins, rows, stations), jnp.bfloat16),
        in_specs=[pl.BlockSpec(memory_space=pltpu.HBM)] * len(operands),
        out_specs=pl.BlockSpec(memory_space=pl.ANY),
        scratch_shapes=[
            pltpu.VMEM((LOADS, stations, segments // LOADS, samples), jnp.bfloat16),
            pltpu.VMEM((segments, stations), jnp.int32),
            pltpu.VMEM((TERMS * 2 * BINS, samples), jnp.bfloat16),
            pltpu.VMEM((samples // 128, stations * segments // LOADS, 128), jnp.float32),
            pltpu.VMEM((BINS * rows, stations), jnp.float32),
            pltpu.VMEM((n_freq, PARTS, bins, rows, stations), jnp.bfloat16),
            pltpu.SemaphoreType.DMA((LOADS + 2,)),
            pltpu.SemaphoreType.DMA((PARTS,)),
            pltpu.SemaphoreType.DMA((count,)),
            pltpu.SemaphoreType.DMA((count,)),
            pltpu.SemaphoreType.DMA((count, n_sta)),
            pltpu.SemaphoreType.DMA((count, n_sta)),
        ],
        compiler_params=pltpu.CompilerParams(
            collective_id=0, has_side_effects=True, vmem_limit_bytes=18 * MIB
        ),
        name="spectra_exchange",
    )(*operands)

    per_step = 4
    scale = 1.0 / (segments * n_freq)
    return pl.pallas_call(
        functools.partial(gram_kernel, per_step, scale),
        out_shape=jax.ShapeDtypeStruct((2, bins, stations, stations * n_sta), jnp.bfloat16),
        grid=(bins // per_step,),
        in_specs=[pl.BlockSpec(memory_space=pltpu.VMEM)],
        out_specs=pl.BlockSpec((2, per_step, stations, stations * n_sta), lambda i: (0, i, 0, 0)),
        compiler_params=pltpu.CompilerParams(vmem_limit_bytes=12 * MIB),
        name="gram",
    )(gathered)


def solution(mesh):
    in_specs = (P("sta", "freq", None), P("sta", "freq"))
    out_specs = P(None, "freq", "sta", None)
    body = functools.partial(shards, mesh.shape["sta"], mesh.shape["freq"])
    return jax.shard_map(body, mesh=mesh, in_specs=in_specs, out_specs=out_specs, check_vma=False)
```

```python
import functools

import jax
import jax.numpy as jnp
import ml_dtypes
import numpy as np
from jax import lax
from jax.experimental import pallas as pl
from jax.experimental.pallas import tpu as pltpu
from jax.sharding import PartitionSpec as P

FFT_LEN = 512
BINS = 128
BAND_LO = 16
PARTS = 4
TERMS = 3
LOADS = 2
HALVES = 2
AHEAD = 2
Z_AHEAD = 6
MESH = pl.DeviceIdType.MESH
MIB = 1 << 20


def spectra_tables():
    t = np.arange(FFT_LEN)
    window = 0.5 - 0.5 * np.cos(2.0 * np.pi * t / FFT_LEN)
    phase = (np.arange(BAND_LO, BAND_LO + BINS)[:, None] * t[None, :] % FFT_LEN) * (2.0 * np.pi / FFT_LEN)
    table = np.concatenate([np.cos(phase), -np.sin(phase)], axis=0) * window
    terms = []
    for _ in range(TERMS):
        terms.append(table.astype(ml_dtypes.bfloat16))
        table = table - terms[-1].astype(np.float64)
    return np.concatenate(terms, axis=0)


def exchange_kernel(
    n_sta, n_freq,
    scale, records, available, table, gathered, early,
    rec, avail, terms, wide, spread, own, rec_sem, keep_sem, zsend, zrecv, send, recv,
):
    me = lax.axis_index("sta")
    z = lax.axis_index("freq")
    stations, load_segs = rec.shape[1], rec.shape[2]
    part_segs = load_segs * LOADS // PARTS
    rows = 2 * part_segs
    bins = BINS // n_freq
    half_bins = bins // HALVES
    mask_bits = [1 << k for k in range(n_sta.bit_length() - 1)]
    far_bits = mask_bits[1:]

    loads = [pltpu.make_async_copy(table, terms, rec_sem.at[LOADS])]
    loads.append(pltpu.make_async_copy(available, avail, rec_sem.at[LOADS + 1]))
    for k in range(LOADS):
        source = records.at[:, pl.ds(k * load_segs, load_segs), :]
        loads.append(pltpu.make_async_copy(source, rec.at[k], rec_sem.at[k]))
    for load in loads:
        load.start()

    barrier = pltpu.get_barrier_semaphore()
    for bit in mask_bits:
        pl.semaphore_signal(barrier, inc=1, device_id=(me ^ bit, z), device_id_type=MESH)
    for step in range(1, n_freq):
        pl.semaphore_signal(barrier, inc=1, device_id=(me, z ^ step), device_id_type=MESH)

    def widen(k):
        def some(block, carry):
            first = pl.multiple_of(block * 16, 16)
            for col in range(FFT_LEN // 128):
                values = rec[k, pl.ds(first, 16), :, pl.ds(col * 128, 128)]
                wide[col, pl.ds(pl.multiple_of(first * load_segs, 256), 16 * load_segs), :] = (
                    values.astype(jnp.float32).reshape(16 * load_segs, 128)
                )
            return carry

        lax.fori_loop(0, stations // 16, some, 0)

    def transform(part):
        offset = part * part_segs % load_segs
        for pair in range(part_segs // 2):
            pieces = []
            for seg in (2 * pair, 2 * pair + 1):
                pieces.append(jnp.concatenate(
                    [wide[col, pl.ds(offset + seg, stations, stride=load_segs), :] for col in range(FFT_LEN // 128)],
                    axis=1,
                ))
            x = jnp.concatenate(pieces, axis=0).astype(jnp.bfloat16)
            contract = (((1,), (1,)), ((), ()))
            sums = lax.dot_general(terms[...], x, contract, preferred_element_type=jnp.float32)
            spectra = sums[(TERMS - 1) * 2 * BINS:]
            for term in range(TERMS - 2, -1, -1):
                spectra = spectra + sums[term * 2 * BINS:(term + 1) * 2 * BINS]
            power = jnp.sum(spectra * spectra, axis=0, keepdims=True) * (1.0 / BINS)
            for k, seg in enumerate((2 * pair, 2 * pair + 1)):
                lanes = slice(k * stations, (k + 1) * stations)
                usable = avail[pl.ds(part * part_segs + seg, 1), :].astype(jnp.float32)
                weight = usable / jnp.sqrt(power[:, lanes] + 1e-05)
                white = spectra[:, lanes] * weight
                spread[pl.ds(seg, BINS, stride=rows), :] = white[:BINS]
                spread[pl.ds(part_segs + seg, BINS, stride=rows), :] = white[BINS:]

        for dest in range(n_freq):
            block = spread[dest * bins * rows:(dest + 1) * bins * rows, :]
            own[dest, :, part] = block.astype(jnp.bfloat16).reshape(HALVES, half_bins, rows, 128)

    chunks = [(0, 0, part, 1) for part in range(PARTS)]
    for half in range(HALVES):
        for step in range(n_freq):
            if (half, step) != (0, 0):
                chunks += [(half, step, part, 2) for part in range(0, PARTS, 2)]
    count = len(chunks)
    first_half = sum(chunk[0] == 0 for chunk in chunks)

    def orders(slot):
        return far_bits if slot % 2 == 0 else far_bits[::-1]

    def piece(slot, mask):
        half, step, part, parts = chunks[slot]
        return gathered.at[me ^ mask, z ^ step, half, pl.ds(part, parts)]

    def forward(slot, mask, bit):
        half, step, part, parts = chunks[slot]
        src = own.at[z, half, pl.ds(part, parts)] if mask == 0 and step == 0 else piece(slot, mask)
        return pltpu.make_async_remote_copy(
            src_ref=src, dst_ref=piece(slot, mask),
            send_sem=send.at[slot, mask ^ bit], recv_sem=recv.at[slot, mask ^ bit],
            device_id=(me ^ bit, z), device_id_type=MESH,
        )

    def arrival(slot, mask):
        here = piece(slot, mask)
        return pltpu.make_async_remote_copy(
            src_ref=here, dst_ref=here, send_sem=send.at[slot, mask], recv_sem=recv.at[slot, mask],
            device_id=(me ^ (mask & -mask), z), device_id_type=MESH,
        )

    def cross(slot):
        half, step, part, parts = chunks[slot]
        return pltpu.make_async_remote_copy(
            src_ref=own.at[z ^ step, half, pl.ds(part, parts)],
            dst_ref=gathered.at[me, z, half, pl.ds(part, parts)],
            send_sem=zsend.at[slot], recv_sem=zrecv.at[slot],
            device_id=(me, z ^ step), device_id_type=MESH,
        )

    def crossed(slot):
        here = piece(slot, 0)
        return pltpu.make_async_remote_copy(
            src_ref=here, dst_ref=here, send_sem=zsend.at[slot], recv_sem=zrecv.at[slot],
            device_id=(me, z ^ chunks[slot][1]), device_id_type=MESH,
        )

    started = []

    def push(slot, mask):
        order = orders(slot)
        last = max([order.index(bit) for bit in order if mask & bit], default=-1)
        for bit in order[last + 1:] + [1]:
            copy = forward(slot, mask, bit)
            copy.start()
            started.append(copy)

    def launch(slot):
        copy = cross(slot)
        copy.start()
        started.append(copy)

    keeps = []
    for part in range(PARTS):
        if part == 0:
            loads[0].wait()
            loads[1].wait()
        if part % (PARTS // LOADS) == 0:
            loads[2 + part * LOADS // PARTS].wait()
            widen(part * LOADS // PARTS)
        transform(part)
        if part == 0:
            pl.semaphore_wait(barrier, len(mask_bits) + n_freq - 1)
        push(part, 0)
        if part % 2 == 1:
            launch(PARTS + part // 2)
        keep = pltpu.make_async_copy(own.at[z, :, part], gathered.at[me, z, :, part], keep_sem.at[part])
        keep.start()
        keeps.append(keep)

    def early_bins(start, stop):
        def one(b, carry):
            gram_bin(
                me, scale, n_sta, n_freq,
                lambda j, zz, part: gathered[j, zz, 0, part, b],
                lambda k, columns, value: early.__setitem__((k, b, slice(None), columns), value),
            )
            return carry

        lax.fori_loop(start, stop, one, 0)

    far_masks = [mask for mask in range(2, n_sta, 2)]
    depth = len(far_bits)
    launched = PARTS + PARTS // 2
    reached = [PARTS] + [0] * depth
    done_bins, turns = None, count + AHEAD + depth + 1
    for turn in range(PARTS, turns):
        while launched < min(count, turn + Z_AHEAD + 1):
            if chunks[launched][1] > 0:
                launch(launched)
            launched += 1
        for lag in range(depth + 1):
            limit = min(count, turn + 1 - (lag + AHEAD if lag else 0))
            for slot in range(reached[lag], limit):
                if lag == 0:
                    if chunks[slot][1] > 0:
                        crossed(slot).wait_recv()
                    push(slot, 0)
                else:
                    for mask in far_masks:
                        if bin(mask).count("1") == lag:
                            arrival(slot, mask).wait_recv()
                            push(slot, mask)
            reached[lag] = max(reached[lag], limit)
        if done_bins is not None and done_bins < half_bins:
            stop = min(half_bins, done_bins + 2)
            early_bins(done_bins, stop)
            done_bins = stop
        if done_bins is None and min(reached) >= first_half:
            for slot in range(first_half):
                for mask in range(1, n_sta, 2):
                    arrival(slot, mask).wait_recv()
            for keep in keeps:
                keep.wait()
            done_bins = 0
    assert min(reached) == count and launched == count
    if done_bins < half_bins:
        early_bins(done_bins, half_bins)

    for slot in range(first_half, count):
        for mask in range(1, n_sta, 2):
            arrival(slot, mask).wait_recv()
    for copy in started:
        copy.wait_send()


def gram_bin(me, scale, n_sta, n_freq, block_of, write):
    places = [(z, part) for z in range(n_freq) for part in range(PARTS)]
    plain, turned = [], []
    for z, part in places:
        block = block_of(me, z, part).astype(jnp.float32) * scale
        half = block.shape[0] // 2
        plain.append(block)
        turned += [block[half:], -block[:half]]
    mine = jnp.concatenate([jnp.concatenate(plain, axis=0), jnp.concatenate(turned, axis=0)], axis=1)
    mine = mine.T.astype(jnp.bfloat16)
    stations = mine.shape[0] // 2
    for j in range(0, n_sta, 2):
        other = jnp.concatenate(
            [jnp.concatenate([block_of(j + k, z, part) for z, part in places], axis=0) for k in (0, 1)], axis=1
        )
        gram = jnp.dot(mine, other, preferred_element_type=jnp.float32).astype(jnp.bfloat16)
        columns = slice(j * stations, (j + 2) * stations)
        write(0, columns, gram[:stations])
        write(1, columns, gram[stations:])


def gram_kernel(per_step, scale, panel, early, out):
    me = lax.axis_index("sta")
    n_sta, n_freq = panel.shape[:2]
    first = pl.program_id(0) * per_step
    for b in range(per_step):
        for k in range(2):
            out[k, 0, b] = early[k, first + b]
        gram_bin(
            me, scale, n_sta, n_freq,
            lambda j, z, part: panel[j, z, 1, part, first + b],
            lambda k, columns, value: out.__setitem__((k, 1, b, slice(None), columns), value),
        )


def shards(n_sta, n_freq, records, available):
    stations, segments, samples = records.shape
    part_segs = segments // PARTS
    rows = 2 * part_segs
    bins = BINS // n_freq
    operands = [records, available.T, jnp.asarray(spectra_tables())]
    operands = [pltpu.with_memory_space_constraint(operand, pltpu.HBM) for operand in operands]
    half_bins = bins // HALVES
    scale = 1.0 / (segments * n_freq)
    count = HALVES * n_freq * PARTS // 2 + PARTS // 2
    gathered, early = pl.pallas_call(
        functools.partial(exchange_kernel, n_sta, n_freq, scale),
        out_shape=(
            jax.ShapeDtypeStruct((n_sta, n_freq, HALVES, PARTS, half_bins, rows, stations), jnp.bfloat16),
            jax.ShapeDtypeStruct((2, half_bins, stations, stations * n_sta), jnp.bfloat16),
        ),
        in_specs=[pl.BlockSpec(memory_space=pltpu.HBM)] * len(operands),
        out_specs=[pl.BlockSpec(memory_space=pltpu.VMEM)] * 2,
        scratch_shapes=[
            pltpu.VMEM((LOADS, stations, segments // LOADS, samples), jnp.bfloat16),
            pltpu.VMEM((segments, stations), jnp.int32),
            pltpu.VMEM((TERMS * 2 * BINS, samples), jnp.bfloat16),
            pltpu.VMEM((samples // 128, stations * segments // LOADS, 128), jnp.float32),
            pltpu.VMEM((BINS * rows, stations), jnp.float32),
            pltpu.VMEM((n_freq, HALVES, PARTS, half_bins, rows, stations), jnp.bfloat16),
            pltpu.SemaphoreType.DMA((LOADS + 2,)),
            pltpu.SemaphoreType.DMA((PARTS,)),
            pltpu.SemaphoreType.DMA((count,)),
            pltpu.SemaphoreType.DMA((count,)),
            pltpu.SemaphoreType.DMA((count, n_sta)),
            pltpu.SemaphoreType.DMA((count, n_sta)),
        ],
        compiler_params=pltpu.CompilerParams(
            collective_id=0, has_side_effects=True, vmem_limit_bytes=13 * MIB
        ),
        name="spectra_exchange",
    )(*operands)

    per_step = 2
    wide = stations * n_sta
    gram = pl.pallas_call(
        functools.partial(gram_kernel, per_step, scale),
        out_shape=jax.ShapeDtypeStruct((2, HALVES, half_bins, stations, wide), jnp.bfloat16),
        grid=(half_bins // per_step,),
        in_specs=[pl.BlockSpec(memory_space=pltpu.VMEM)] * 2,
        out_specs=pl.BlockSpec((2, HALVES, per_step, stations, wide), lambda i: (0, 0, i, 0, 0)),
        compiler_params=pltpu.CompilerParams(vmem_limit_bytes=11 * MIB),
        name="gram",
    )(gathered, early)
    return gram.reshape(2, bins, stations, wide)


def solution(mesh):
    in_specs = (P("sta", "freq", None), P("sta", "freq"))
    out_specs = P(None, "freq", "sta", None)
    body = functools.partial(shards, mesh.shape["sta"], mesh.shape["freq"])
    return jax.shard_map(body, mesh=mesh, in_specs=in_specs, out_specs=out_specs, check_vma=False)
```

```python
import functools

import jax
import jax.numpy as jnp
import ml_dtypes
import numpy as np
from jax import lax
from jax.experimental import pallas as pl
from jax.experimental.pallas import tpu as pltpu
from jax.sharding import PartitionSpec as P

FFT_LEN = 512
BINS = 128
BAND_LO = 16
PARTS = 4
TERMS = 3
LOADS = 2
AHEAD = 4
Z_AHEAD = 6
MESH = pl.DeviceIdType.MESH
MIB = 1 << 20


def spectra_tables():
    t = np.arange(FFT_LEN)
    window = 0.5 - 0.5 * np.cos(2.0 * np.pi * t / FFT_LEN)
    phase = (np.arange(BAND_LO, BAND_LO + BINS)[:, None] * t[None, :] % FFT_LEN) * (2.0 * np.pi / FFT_LEN)
    table = np.concatenate([np.cos(phase), -np.sin(phase)], axis=0) * window
    terms = []
    for _ in range(TERMS):
        terms.append(table.astype(ml_dtypes.bfloat16))
        table = table - terms[-1].astype(np.float64)
    return np.concatenate(terms, axis=0)


def exchange_kernel(
    n_sta, n_freq,
    records, available, table, gathered,
    rec, avail, terms, wide, spread, own, rec_sem, keep_sem, zsend, zrecv, send, recv,
):
    me = lax.axis_index("sta")
    z = lax.axis_index("freq")
    stations, load_segs = rec.shape[1], rec.shape[2]
    part_segs = load_segs * LOADS // PARTS
    rows = 2 * part_segs
    bins = BINS // n_freq
    mask_bits = [1 << k for k in range(n_sta.bit_length() - 1)]
    far_bits = mask_bits[1:]

    loads = [pltpu.make_async_copy(table, terms, rec_sem.at[LOADS])]
    loads.append(pltpu.make_async_copy(available, avail, rec_sem.at[LOADS + 1]))
    for k in range(LOADS):
        source = records.at[:, pl.ds(k * load_segs, load_segs), :]
        loads.append(pltpu.make_async_copy(source, rec.at[k], rec_sem.at[k]))
    for load in loads:
        load.start()

    barrier = pltpu.get_barrier_semaphore()
    for bit in mask_bits:
        pl.semaphore_signal(barrier, inc=1, device_id=(me ^ bit, z), device_id_type=MESH)
    for step in range(1, n_freq):
        pl.semaphore_signal(barrier, inc=1, device_id=(me, z ^ step), device_id_type=MESH)

    def widen(k):
        def some(block, carry):
            first = pl.multiple_of(block * 16, 16)
            for col in range(FFT_LEN // 128):
                values = rec[k, pl.ds(first, 16), :, pl.ds(col * 128, 128)]
                wide[col, pl.ds(pl.multiple_of(first * load_segs, 256), 16 * load_segs), :] = (
                    values.astype(jnp.float32).reshape(16 * load_segs, 128)
                )
            return carry

        lax.fori_loop(0, stations // 16, some, 0)

    def transform(part):
        offset = part * part_segs % load_segs
        for pair in range(part_segs // 2):
            pieces = []
            for seg in (2 * pair, 2 * pair + 1):
                pieces.append(jnp.concatenate(
                    [wide[col, pl.ds(offset + seg, stations, stride=load_segs), :] for col in range(FFT_LEN // 128)],
                    axis=1,
                ))
            x = jnp.concatenate(pieces, axis=0).astype(jnp.bfloat16)
            contract = (((1,), (1,)), ((), ()))
            sums = lax.dot_general(terms[...], x, contract, preferred_element_type=jnp.float32)
            spectra = sums[(TERMS - 1) * 2 * BINS:]
            for term in range(TERMS - 2, -1, -1):
                spectra = spectra + sums[term * 2 * BINS:(term + 1) * 2 * BINS]
            power = jnp.sum(spectra * spectra, axis=0, keepdims=True) * (1.0 / BINS)
            for k, seg in enumerate((2 * pair, 2 * pair + 1)):
                lanes = slice(k * stations, (k + 1) * stations)
                usable = avail[pl.ds(part * part_segs + seg, 1), :].astype(jnp.float32)
                weight = usable / jnp.sqrt(power[:, lanes] + 1e-05)
                white = spectra[:, lanes] * weight
                spread[pl.ds(seg, BINS, stride=rows), :] = white[:BINS]
                spread[pl.ds(part_segs + seg, BINS, stride=rows), :] = white[BINS:]

        for dest in range(n_freq):
            block = spread[dest * bins * rows:(dest + 1) * bins * rows, :]
            own[dest, part] = block.astype(jnp.bfloat16).reshape(bins, rows, 128)

    def orders(part):
        return far_bits if part % 2 == 0 else far_bits[::-1]

    def piece(step, part, mask):
        return gathered.at[me ^ mask, z ^ step, part]

    def forward(step, part, mask, bit):
        src = own.at[z, part] if mask == 0 and step == 0 else piece(step, part, mask)
        return pltpu.make_async_remote_copy(
            src_ref=src, dst_ref=piece(step, part, mask),
            send_sem=send.at[step * PARTS + part, mask ^ bit], recv_sem=recv.at[step * PARTS + part, mask ^ bit],
            device_id=(me ^ bit, z), device_id_type=MESH,
        )

    def arrival(step, part, mask):
        here = piece(step, part, mask)
        return pltpu.make_async_remote_copy(
            src_ref=here, dst_ref=here,
            send_sem=send.at[step * PARTS + part, mask], recv_sem=recv.at[step * PARTS + part, mask],
            device_id=(me ^ (mask & -mask), z), device_id_type=MESH,
        )

    def cross(step, part):
        return pltpu.make_async_remote_copy(
            src_ref=own.at[z ^ step, part], dst_ref=gathered.at[me, z, part],
            send_sem=zsend.at[step * PARTS + part], recv_sem=zrecv.at[step * PARTS + part],
            device_id=(me, z ^ step), device_id_type=MESH,
        )

    def crossed(step, part):
        here = piece(step, part, 0)
        return pltpu.make_async_remote_copy(
            src_ref=here, dst_ref=here,
            send_sem=zsend.at[step * PARTS + part], recv_sem=zrecv.at[step * PARTS + part],
            device_id=(me, z ^ step), device_id_type=MESH,
        )

    started = []

    def push(step, part, mask):
        order = orders(part)
        last = max([order.index(bit) for bit in order if mask & bit], default=-1)
        for bit in order[last + 1:] + [1]:
            copy = forward(step, part, mask, bit)
            copy.start()
            started.append(copy)

    def launch(step, part):
        copy = cross(step, part)
        copy.start()
        started.append(copy)

    keeps = []
    for part in range(PARTS):
        if part == 0:
            loads[0].wait()
            loads[1].wait()
        if part % (PARTS // LOADS) == 0:
            loads[2 + part * LOADS // PARTS].wait()
            widen(part * LOADS // PARTS)
        transform(part)
        if part == 0:
            pl.semaphore_wait(barrier, len(mask_bits) + n_freq - 1)
        push(0, part, 0)
        launch(1, part)
        keep = pltpu.make_async_copy(own.at[z, part], gathered.at[me, z, part], keep_sem.at[part])
        keep.start()
        keeps.append(keep)

    far_masks = [mask for mask in range(2, n_sta, 2)]
    count = n_freq * PARTS
    depth = len(far_bits)
    launched = 2 * PARTS
    reached = [PARTS] + [0] * depth
    for turn in range(PARTS, count + AHEAD + depth + 1):
        while launched < min(count, turn + Z_AHEAD + 1):
            launch(*divmod(launched, PARTS))
            launched += 1
        for lag in range(depth + 1):
            limit = min(count, turn + 1 - (lag + AHEAD if lag else 0))
            for slot in range(reached[lag], limit):
                step, part = divmod(slot, PARTS)
                if lag == 0:
                    crossed(step, part).wait_recv()
                    push(step, part, 0)
                else:
                    for mask in far_masks:
                        if bin(mask).count("1") == lag:
                            arrival(step, part, mask).wait_recv()
                            push(step, part, mask)
            reached[lag] = max(reached[lag], limit)
    assert min(reached) == count and launched == count

    for slot in range(count):
        step, part = divmod(slot, PARTS)
        for mask in range(1, n_sta, 2):
            arrival(step, part, mask).wait_recv()
    for keep in keeps:
        keep.wait()
    for copy in started:
        copy.wait_send()


def gram_kernel(per_step, scale, panel, out):
    me = lax.axis_index("sta")
    n_sta, n_freq, parts, _, rows, _ = panel.shape
    half = rows // 2
    first = pl.program_id(0) * per_step
    places = [(z, part) for z in range(n_freq) for part in range(parts)]
    stations = out.shape[2]
    wide = 2 * stations
    for b in range(per_step):
        plain, turned = [], []
        for z, part in places:
            block = panel[me, z, part, first + b].astype(jnp.float32) * scale
            plain.append(block)
            turned += [block[half:], -block[:half]]
        mine = jnp.concatenate([jnp.concatenate(plain, axis=0), jnp.concatenate(turned, axis=0)], axis=1)
        mine = mine.T.astype(jnp.bfloat16)
        for j in range(0, n_sta, 2):
            other = jnp.concatenate(
                [jnp.concatenate([panel[j + k, z, part, first + b] for z, part in places], axis=0) for k in (0, 1)],
                axis=1,
            )
            gram = jnp.dot(mine, other, preferred_element_type=jnp.float32).astype(jnp.bfloat16)
            columns = slice(j * stations, j * stations + wide)
            out[0, b, :, columns] = gram[:stations]
            out[1, b, :, columns] = gram[stations:]


def shards(n_sta, n_freq, records, available):
    stations, segments, samples = records.shape
    part_segs = segments // PARTS
    rows = 2 * part_segs
    bins = BINS // n_freq
    operands = [records, available.T, jnp.asarray(spectra_tables())]
    operands = [pltpu.with_memory_space_constraint(operand, pltpu.HBM) for operand in operands]
    count = n_freq * PARTS
    gathered = pl.pallas_call(
        functools.partial(exchange_kernel, n_sta, n_freq),
        out_shape=jax.ShapeDtypeStruct((n_sta, n_freq, PARTS, bins, rows, stations), jnp.bfloat16),
        in_specs=[pl.BlockSpec(memory_space=pltpu.HBM)] * len(operands),
        out_specs=pl.BlockSpec(memory_space=pl.ANY),
        scratch_shapes=[
            pltpu.VMEM((LOADS, stations, segments // LOADS, samples), jnp.bfloat16),
            pltpu.VMEM((segments, stations), jnp.int32),
            pltpu.VMEM((TERMS * 2 * BINS, samples), jnp.bfloat16),
            pltpu.VMEM((samples // 128, stations * segments // LOADS, 128), jnp.float32),
            pltpu.VMEM((BINS * rows, stations), jnp.float32),
            pltpu.VMEM((n_freq, PARTS, bins, rows, stations), jnp.bfloat16),
            pltpu.SemaphoreType.DMA((LOADS + 2,)),
            pltpu.SemaphoreType.DMA((PARTS,)),
            pltpu.SemaphoreType.DMA((count,)),
            pltpu.SemaphoreType.DMA((count,)),
            pltpu.SemaphoreType.DMA((count, n_sta)),
            pltpu.SemaphoreType.DMA((count, n_sta)),
        ],
        compiler_params=pltpu.CompilerParams(
            collective_id=0, has_side_effects=True, vmem_limit_bytes=18 * MIB
        ),
        name="spectra_exchange",
    )(*operands)

    per_step = 2
    scale = 1.0 / (segments * n_freq)
    return pl.pallas_call(
        functools.partial(gram_kernel, per_step, scale),
        out_shape=jax.ShapeDtypeStruct((2, bins, stations, stations * n_sta), jnp.bfloat16),
        grid=(bins // per_step,),
        in_specs=[pl.BlockSpec(memory_space=pltpu.VMEM)],
        out_specs=pl.BlockSpec((2, per_step, stations, stations * n_sta), lambda i: (0, i, 0, 0)),
        compiler_params=pltpu.CompilerParams(vmem_limit_bytes=12 * MIB),
        name="gram",
    )(gathered)


def solution(mesh):
    in_specs = (P("sta", "freq", None), P("sta", "freq"))
    out_specs = P(None, "freq", "sta", None)
    body = functools.partial(shards, mesh.shape["sta"], mesh.shape["freq"])
    return jax.shard_map(body, mesh=mesh, in_specs=in_specs, out_specs=out_specs, check_vma=False)
```
